32 devices in a mesh: group: 8 (over z, x), local: 4 (over y, core).
Axes of the slice: x: 2, y: 2, z: 4, core: 2. Of those that a mesh axis runs over, the one named last changes fastest.
Arguments:
- tokens: bfloat16 [512, 3584], P(('group', 'local')), may hold values from -6 to 6
- expert_ids: int32 [512, 8], P(('group', 'local')), may hold values from 0 to 31, as said below
- gate_codes: int32 [512, 8], P(('group', 'local')), may hold values from 1 to 1024
- w_gate: bfloat16 [32, 3584, 1024], P(('group', 'local')), may hold values from -0.09375 to 0.09375
- w_up: bfloat16 [32, 3584, 1024], P(('group', 'local')), may hold values from -0.09375 to 0.09375
- w_down: bfloat16 [32, 1024, 3584], P(('group', 'local')), may hold values from -0.1875 to 0.1875
Outputs:
- mixed: bfloat16 [512, 3584], P(('group', 'local'))
The draws below stay inside these ranges and needn't reach their ends.
Inputs may be any that keep to these rules, and one draw needn't show every extreme that they name: `expert_ids`: each row names 8 different experts, and they lie within at most 4 node groups, node group g holding experts g * 4 to (g + 1) * 4 - 1.
All inputs are finite; a program needn't handle non-finite values.
Results may differ from the reference program's by a relative error of at most 0.0057.
Values may be sent and summed in bfloat16 or wider, within the bound.
A program may use at most 128 MiB of HBM per device.

```python
import jax
import jax.numpy as jnp
from jax import lax

D = 3584
H = 1024
TOPK = 8
TOPG = 4
TOK_DEV = 16
EXPERTS = 32
EXP_GROUP = 4
CAP = 8
TOKENS = 512
N_GROUP = 8
N_LOCAL = 4


def draw_expert_ids(key, part):
    base = jax.random.fold_in(key, 11)
    key_pop, key_gpop, key_group, key_expert = jax.random.split(base, 4)
    groups = EXPERTS // EXP_GROUP
    popular = jax.random.randint(key_pop, (EXPERTS,), 1, 5)
    group_pop = jax.random.randint(key_gpop, (groups,), 1, 4)
    group_score = jax.random.randint(key_group, (TOKENS, groups), 0, 4096) * group_pop[None, :]
    group_score = group_score * groups + jnp.arange(groups, dtype=jnp.int32)[None, :]
    unused, chosen = lax.top_k(group_score, TOPG)
    group_range = jnp.arange(groups, dtype=jnp.int32)
    group_mask = jnp.any(chosen[:, :, None] == group_range[None, None, :], axis=1)
    expert_range = jnp.arange(EXPERTS, dtype=jnp.int32)
    allowed = group_mask[:, expert_range // EXP_GROUP]
    expert_score = jax.random.randint(key_expert, (TOKENS, EXPERTS), 0, 4096) * popular[None, :]
    expert_score = expert_score * EXPERTS + expert_range[None, :]
    expert_score = jnp.where(allowed, expert_score, -1 - expert_range[None, :])
    unused_two, picked = lax.top_k(expert_score, TOPK)
    return picked.astype(jnp.int32)


def touch_ends(values, stream_key, smallest, high):
    dims = values.shape
    spot = [jax.random.randint(jax.random.fold_in(stream_key, axis), (), 0, dims[axis]) for axis in range(len(dims))]
    values = values.at[tuple(spot)].set(smallest)
    longest = dims.index(max(dims))
    spot[longest] = (spot[longest] + 1) % dims[longest]
    return values.at[tuple(spot)].set(high)


def steps_of(own_key, extent, cuts, low, largest):
    def one(position, blocks):
        steps = jax.random.uniform(jax.random.fold_in(jax.random.fold_in(own_key, 6), position), (blocks,), jnp.float32, low / len(cuts), largest / len(cuts))
        return jnp.repeat(jnp.exp(steps), extent[position] // blocks).reshape((-1,) + (1,) * (len(extent) - position - 1))

    loudness = one(*cuts[0])
    for cut in cuts[1:]:
        loudness = loudness * one(*cut)
    return loudness


def centred(rng, extent, spread, reach, shards=(), held_as=jnp.bfloat16):
    values = spread * jax.random.normal(rng, extent, jnp.float32)
    if shards:
        values = values * steps_of(rng, extent, shards, -0.22, 0.18)
    return jnp.clip(values, -reach, reach).astype(held_as)


def setup_inputs(seed: int = 0) -> dict:
    key_list = jax.random.split(jax.random.key(seed), 7)
    return {
        "tokens": centred(key_list[0], (TOKENS, D), 1.0, 6.0, ((0, 32),)),
        "expert_ids": draw_expert_ids(jax.random.fold_in(key_list[6], 71), 0),
        "gate_codes": touch_ends(jax.random.randint(key_list[2], (TOKENS, TOPK), 1, 1025), jax.random.fold_in(key_list[2], 1), 1, 1024).astype(jnp.int32),
        "w_gate": centred(key_list[3], (EXPERTS, D, H), D ** -0.5, 0.09375, ((0, 32),)),
        "w_up": centred(key_list[4], (EXPERTS, D, H), D ** -0.5, 0.09375, ((0, 32),)),
        "w_down": centred(key_list[5], (EXPERTS, H, D), H ** -0.5, 0.1875, ((0, 32),)),
    }


def reference(tokens, expert_ids, gate_codes, w_gate, w_up, w_down):
    devices = N_GROUP * N_LOCAL
    block_ids = expert_ids.reshape(devices, TOK_DEV, TOPK)
    expert_range = jnp.arange(EXPERTS, dtype=jnp.int32)
    onehot = (block_ids[:, :, :, None] == expert_range[None, None, None, :]).astype(jnp.int32)
    present = jnp.sum(onehot, axis=2)
    before = jnp.cumsum(present, axis=1) - present
    slot_rank = jnp.sum(onehot * before[:, :, None, :], axis=3)
    kept = slot_rank < CAP
    device_index = jnp.arange(devices, dtype=jnp.int32)[:, None, None]
    total_slots = EXPERTS * devices * CAP
    slot_index = jnp.where(kept, block_ids * (devices * CAP) + device_index * CAP + slot_rank, total_slots).astype(jnp.int32)
    token_index = jnp.broadcast_to(device_index * TOK_DEV + jnp.arange(TOK_DEV, dtype=jnp.int32)[None, :, None], block_ids.shape).astype(jnp.int32)
    flat_index = slot_index.reshape(-1)
    slot_token = jnp.zeros((total_slots,), jnp.int32).at[flat_index].set(token_index.reshape(-1), mode="drop")
    slot_live = jnp.zeros((total_slots,), jnp.bool_).at[flat_index].set(True, mode="drop")

    def one_expert(operands):
        table, live, gate_mat, up_mat, down_mat = operands
        rows = jnp.where(live[:, None], tokens[table], jnp.zeros((), tokens.dtype))
        gate_part = jnp.dot(rows, gate_mat, preferred_element_type=jnp.float32)
        up_part = jnp.dot(rows, up_mat, preferred_element_type=jnp.float32)
        hidden = (jax.nn.silu(gate_part) * up_part).astype(jnp.bfloat16)
        result = jnp.dot(hidden, down_mat, preferred_element_type=jnp.float32).astype(jnp.bfloat16)
        return jnp.where(live[:, None], result, jnp.zeros((), jnp.bfloat16))

    expert_out = lax.map(one_expert, (slot_token.reshape(EXPERTS, devices * CAP), slot_live.reshape(EXPERTS, devices * CAP), w_gate, w_up, w_down))
    flat_out = expert_out.reshape(total_slots, D)
    picked = flat_out[jnp.minimum(flat_index, total_slots - 1)].reshape(TOKENS, TOPK, D)
    weight = jnp.where(kept.reshape(TOKENS, TOPK), gate_codes.astype(jnp.float32) / 1024.0, jnp.zeros((), jnp.float32))
    mixed = jnp.sum(weight[:, :, None] * picked.astype(jnp.float32), axis=1)
    return mixed.astype(jnp.bfloat16)
```

```python
import functools

import jax
import jax.numpy as jnp
from jax import lax
from jax.experimental import pallas as pl
from jax.experimental.pallas import tpu as pltpu
from jax.sharding import PartitionSpec as P

BF = jnp.bfloat16
F32 = jnp.float32
NZ = 4
CORES = 2
GATHER_LAG = (0, 1, 2, 3)
SUM_LAG = (1, 3, 4, 5)


def widths_of(width):
    unit = 512
    count = width // unit
    sizes = [unit] * (count - 1) + [unit // 2, unit // 2]
    return sizes


class Plan:
    def __init__(self, groups, locals_, rows, width, hidden, top):
        self.sizes = {"z": NZ, "x": groups // NZ, "y": locals_ // CORES, "c": CORES}
        self.groups, self.locals = groups, locals_
        self.devices = groups * locals_
        self.rows, self.width, self.hidden, self.top = rows, width, hidden, top
        self.cap = 2 * rows * top // self.devices
        self.widths = widths_of(width)
        self.chunks = len(self.widths)
        self.starts = [sum(self.widths[:c]) for c in range(self.chunks)]
        self.tokens = rows * self.devices
        self.half = self.tokens // CORES
        self.slots = self.devices // CORES * self.cap
        self.table = -(-3 * self.devices // 128) * 128
        self.peers = max(self.sizes.values()) - 1

    def order(self, chunk):
        return "zxyc" if chunk % 2 == 0 else "zyxc"

    def buffer_width(self, chunk):
        return self.widths[chunk] + (self.table if chunk < 2 else 0)

    def steps(self, chunk):
        out, step = [], 1
        for axis in self.order(chunk):
            out.append((axis, self.sizes[axis], step))
            step *= self.sizes[axis]
        return out


def bits(number):
    return number.bit_length() - 1


def kernel(plan, tok, ids, codes, wg, wu, wd, out, *scratch):
    p = plan
    nc = p.chunks
    rows = p.rows
    scratch = list(scratch)
    xbuf = [scratch.pop(0) for _ in range(nc)]
    rbuf = [[scratch.pop(0) for _ in range(4)] for _ in range(nc)]
    (gate_v, up_v, down_v, picked, gate_acc, up_acc, hid, scat, gath, slot_w, weighted,
     ag_send, ag_recv, rs_send, rs_recv, w_sem) = scratch

    g = lax.axis_index("group")
    l = lax.axis_index("local")
    me = g * p.locals + l
    nx = p.sizes["x"]
    at = {"z": g // nx, "x": g % nx, "y": l // CORES, "c": l % CORES}

    def peer(axis, k):
        spot = dict(at)
        spot[axis] = lax.rem(at[axis] + k, p.sizes[axis])
        return (spot["z"] * nx + spot["x"], spot["y"] * CORES + spot["c"]), spot[axis]

    loads = []
    for c in range(nc):
        span = pl.ds(p.starts[c], p.widths[c])
        pair = (
            pltpu.make_async_copy(wg.at[0, span, :], gate_v.at[span, :], w_sem.at[0, c]),
            pltpu.make_async_copy(wu.at[0, span, :], up_v.at[span, :], w_sem.at[1, c]),
        )
        for copy in pair:
            copy.start()
        loads.append(pair)
    down_load = pltpu.make_async_copy(wd.at[0], down_v, w_sem.at[2, 0])
    down_load.start()

    barrier = pltpu.get_barrier_semaphore()
    greeted = 0
    for axis in "zxyc":
        for k in range(1, p.sizes[axis]):
            pl.semaphore_signal(
                barrier, inc=1, device_id=peer(axis, k)[0], device_id_type=pl.DeviceIdType.MESH
            )
            greeted += 1

    lane = lax.broadcasted_iota(jnp.int32, (rows, p.table), 1)
    which = lane & (p.devices - 1)
    part = lane >> bits(p.devices)
    present = jnp.zeros((rows, p.table), F32)
    code = jnp.zeros((rows, p.table), jnp.int32)
    for k in range(p.top):
        hit = ids[:, k : k + 1] == which
        present = jnp.where(hit, 1.0, present)
        code = jnp.where(hit, codes[:, k : k + 1], code)
    earlier = lax.broadcasted_iota(jnp.int32, (rows, rows), 0) > lax.broadcasted_iota(
        jnp.int32, (rows, rows), 1
    )
    before = jnp.dot(
        jnp.where(earlier, 1.0, 0.0).astype(BF), present.astype(BF), preferred_element_type=F32
    )
    live = jnp.logical_and(present > 0.5, before < p.cap - 0.5)
    rank = jnp.where(live, before, -1.0)
    high = jnp.where(live, (code >> 5).astype(F32), 0.0)
    low = jnp.where(live, (code & 31).astype(F32), 0.0)
    table = jnp.where(part == 0, rank, jnp.where(part == 1, high, low)).astype(BF)

    def base(c, j):
        total = 0
        for axis, size, step in p.steps(c)[j:]:
            total = total + at[axis] * step
        return total

    def span_of(start, count):
        return pl.ds(pl.multiple_of(start * rows, 16), count * rows)

    for c in range(nc):
        own = span_of(base(c, 0), 1)
        xbuf[c][own, : p.widths[c]] = tok[:, p.starts[c] : p.starts[c] + p.widths[c]]
        if c < 2:
            xbuf[c][own, p.widths[c] :] = table

    pl.semaphore_wait(barrier, greeted)

    def gather_copies(c, j):
        axis, size, step = p.steps(c)[j]
        span = span_of(base(c, j), step)
        copies = []
        for k in range(1, size):
            copies.append(
                pltpu.make_async_remote_copy(
                    src_ref=xbuf[c].at[span, :],
                    dst_ref=xbuf[c].at[span, :],
                    send_sem=ag_send.at[c, j, k - 1],
                    recv_sem=ag_recv.at[c, j, k - 1],
                    device_id=peer(axis, k)[0],
                    device_id_type=pl.DeviceIdType.MESH,
                )
            )
        return copies

    gathers = {}

    def gather_start(c, j):
        gathers[c, j] = gather_copies(c, j)
        for copy in gathers[c, j]:
            copy.start()

    def gather_wait(c, j):
        for copy in gathers[c, j]:
            copy.wait_recv()

    def one_hots(par):
        order = p.order(par)
        wide = p.widths[par]
        for core in range(CORES):
            tab = xbuf[par][core * p.half : (core + 1) * p.half, wide:].astype(F32)
            lanes = lax.broadcasted_iota(jnp.int32, (p.half, p.table), 1)
            rk = jnp.sum(jnp.where(lanes == me, tab, 0.0), axis=1, keepdims=True)
            row = lax.broadcasted_iota(jnp.int32, (p.half, p.slots), 0) >> bits(rows)
            spot = {}
            for axis in order[:3]:
                spot[axis] = row & (p.sizes[axis] - 1)
                row = row >> bits(p.sizes[axis])
            canon = (spot["y"] * p.sizes["x"] + spot["x"]) * p.sizes["z"] + spot["z"]
            slot = lax.broadcasted_iota(jnp.int32, (p.half, p.slots), 1)
            gap = (slot - canon * p.cap).astype(F32)
            hot = jnp.where(jnp.logical_and(gap == rk, rk > -0.5), 1.0, 0.0)
            scat[par, core * p.half : (core + 1) * p.half, :] = hot.astype(BF)
            turned = hot.T.astype(BF)
            gath[par, core] = turned
            if par == 0:
                tabs = jnp.dot(
                    turned,
                    xbuf[par][core * p.half : (core + 1) * p.half, wide:],
                    preferred_element_type=F32,
                )
                lanes = lax.broadcasted_iota(jnp.int32, (p.slots, p.table), 1)
                gate = jnp.where(lanes == p.devices + me, tabs * 32.0, 0.0)
                gate = gate + jnp.where(lanes == 2 * p.devices + me, tabs, 0.0)
                gate = jnp.sum(gate, axis=1, keepdims=True) * (1.0 / 1024.0)
                slot_w[core * p.slots : (core + 1) * p.slots, :] = jnp.broadcast_to(
                    gate, (p.slots, 128)
                )

    def into_hidden(c):
        par, wide = c % 2, p.widths[c]
        if c < 2:
            one_hots(par)
        for core in range(CORES):
            got = jnp.dot(
                gath[par, core],
                xbuf[c][core * p.half : (core + 1) * p.half, :wide],
                preferred_element_type=F32,
            )
            picked[core * p.slots : (core + 1) * p.slots, :wide] = got.astype(BF)
        for copy in loads[c]:
            copy.wait()
        depth = pl.ds(p.starts[c], wide)

        def tile(n, carry):
            cols = pl.ds(pl.multiple_of(n * 256, 256), 256)
            lhs = picked[:, :wide]
            a = jnp.dot(lhs, gate_v[depth, cols], preferred_element_type=F32)
            b = jnp.dot(lhs, up_v[depth, cols], preferred_element_type=F32)
            if c > 0:
                a = a + gate_acc[:, cols]
                b = b + up_acc[:, cols]
            if c == nc - 1:
                hid[:, cols] = (a / (1.0 + jnp.exp(-a)) * b).astype(BF)
            else:
                gate_acc[:, cols] = a
                up_acc[:, cols] = b
            return carry

        lax.fori_loop(0, p.hidden // 256, tile, 0)

    for c in range(nc):
        gather_start(c, 0)
    for t in range(nc + GATHER_LAG[3]):
        for j in (1, 2, 3):
            c = t - GATHER_LAG[j - 1]
            if 0 <= c < nc:
                gather_wait(c, j - 1)
                gather_start(c, j)
        c = t - GATHER_LAG[3]
        if 0 <= c < nc:
            gather_wait(c, 3)
            into_hidden(c)

    for c in range(nc):
        for j in range(4):
            for copy in gathers[c, j]:
                copy.wait_send()
    down_load.wait()

    sums = {}

    def sum_start(c, j):
        axis, size, step = p.steps(c)[j]
        outer = base(c, j + 1)
        copies = []
        for k in range(1, size):
            device, spot = peer(axis, k)
            copies.append(
                pltpu.make_async_remote_copy(
                    src_ref=xbuf[c].at[span_of(outer + spot * step, step), pl.ds(0, p.widths[c])],
                    dst_ref=rbuf[c][j].at[k - 1],
                    send_sem=rs_send.at[c, j, k - 1],
                    recv_sem=rs_recv.at[c, j, k - 1],
                    device_id=device,
                    device_id_type=pl.DeviceIdType.MESH,
                )
            )
        for copy in copies:
            copy.start()
        sums[c, j] = copies

    def sum_finish(c, j):
        axis, size, step = p.steps(c)[j]
        wide = p.widths[c]
        for copy in sums[c, j]:
            copy.wait_recv()
        start = base(c, j) * rows
        if j == 0:
            span = pl.ds(pl.multiple_of(start, 16), rows)
            total = xbuf[c][span, :wide].astype(F32)
            for k in range(size - 1):
                total = total + rbuf[c][j][k].astype(F32)
            out[:, p.starts[c] : p.starts[c] + wide] = total.astype(BF)
            return
        block = min(step * rows, 64)

        def add(i, carry):
            span = pl.ds(pl.multiple_of(start + i * block, 16), block)
            inner = pl.ds(pl.multiple_of(i * block, 16), block)
            if size == 2:
                xbuf[c][span, :wide] = xbuf[c][span, :wide] + rbuf[c][j][0, inner, :]
            else:
                total = xbuf[c][span, :wide].astype(F32)
                for k in range(size - 1):
                    total = total + rbuf[c][j][k, inner, :].astype(F32)
                xbuf[c][span, :wide] = total.astype(BF)
            return carry

        lax.fori_loop(0, step * rows // block, add, 0)

    def out_of_hidden(c):
        par, wide = c % 2, p.widths[c]

        def tile(n, carry):
            source = pl.ds(pl.multiple_of(p.starts[c] + n * 256, 256), 256)
            cols = pl.ds(pl.multiple_of(n * 256, 256), 256)
            made = jnp.dot(hid[...], down_v[:, source], preferred_element_type=F32)
            made = made * slot_w[:, :1]
            weighted[...] = made.astype(BF)
            for core in range(CORES):
                spread = jnp.dot(
                    scat[par, core * p.half : (core + 1) * p.half, :],
                    weighted[core * p.slots : (core + 1) * p.slots, :],
                    preferred_element_type=F32,
                )
                xbuf[c][core * p.half : (core + 1) * p.half, cols] = spread.astype(BF)
            return carry

        lax.fori_loop(0, wide // 256, tile, 0)

    for t in range(nc + SUM_LAG[3]):
        if t < nc:
            out_of_hidden(t)
            sum_start(t, 3)
        for lag, j in zip(SUM_LAG, (3, 2, 1, 0)):
            c = t - lag
            if 0 <= c < nc:
                sum_finish(c, j)
                if j > 0:
                    sum_start(c, j - 1)
    for c in range(nc):
        for j in range(4):
            for copy in sums[c, j]:
                copy.wait_send()


def local(tokens, expert_ids, gate_codes, w_gate, w_up, w_down):
    rows, width = tokens.shape
    hidden = w_gate.shape[2]
    p = Plan(
        lax.axis_size("group"), lax.axis_size("local"), rows, width, hidden, expert_ids.shape[1]
    )
    nc = p.chunks
    wide = max(p.widths)
    shapes = [pltpu.VMEM((p.tokens, p.buffer_width(c)), BF) for c in range(nc)]
    for c in range(nc):
        for axis, size, step in p.steps(c):
            shapes.append(pltpu.VMEM((size - 1, step * rows, p.widths[c]), BF))
    slots = CORES * p.slots
    sems = pltpu.SemaphoreType.DMA((nc, 4, p.peers))
    shapes += [
        pltpu.VMEM((width, hidden), BF),
        pltpu.VMEM((width, hidden), BF),
        pltpu.VMEM((hidden, width), BF),
        pltpu.VMEM((slots, wide), BF),
        pltpu.VMEM((slots, hidden), F32),
        pltpu.VMEM((slots, hidden), F32),
        pltpu.VMEM((slots, hidden), BF),
        pltpu.VMEM((2, p.tokens, p.slots), BF),
        pltpu.VMEM((2, CORES, p.slots, p.half), BF),
        pltpu.VMEM((slots, 128), F32),
        pltpu.VMEM((slots, 256), BF),
        sems, sems, sems, sems,
        pltpu.SemaphoreType.DMA((3, nc)),
    ]
    vmem = pl.BlockSpec(memory_space=pltpu.VMEM)
    hbm = pl.BlockSpec(memory_space=pl.ANY)
    return pl.pallas_call(
        functools.partial(kernel, p),
        out_shape=jax.ShapeDtypeStruct((rows, width), BF),
        in_specs=[vmem, vmem, vmem, hbm, hbm, hbm],
        out_specs=vmem,
        scratch_shapes=shapes,
        compiler_params=pltpu.CompilerParams(
            collective_id=0, has_side_effects=True, vmem_limit_bytes=62 * 1024 * 1024
        ),
        cost_estimate=pl.CostEstimate(
            flops=6 * slots * width * hidden, bytes_accessed=6 * width * hidden, transcendentals=0
        ),
    )(tokens, expert_ids, gate_codes, w_gate, w_up, w_down)


def solution(mesh):
    placed = (
        P(("group", "local"), None),
        P(("group", "local"), None),
        P(("group", "local"), None),
        P(("group", "local"), None, None),
        P(("group", "local"), None, None),
        P(("group", "local"), None, None),
    )
    return jax.shard_map(
        local, mesh=mesh, in_specs=placed, out_specs=P(("group", "local"), None), check_vma=False
    )
```

```python
import functools

import jax
import jax.numpy as jnp
from jax import lax
from jax.experimental import pallas as pl
from jax.experimental.pallas import tpu as pltpu
from jax.sharding import PartitionSpec as P

BF = jnp.bfloat16
F32 = jnp.float32
NZ = 4
CORES = 2
GATHER_LAG = (0, 2, 4, 5)
SUM_LAG = (2, 4, 6, 8)


def widths_of(width):
    unit = 512
    count = width // unit
    sizes = [unit] * (count - 1) + [unit // 2, unit // 2]
    return sizes


class Plan:
    def __init__(self, groups, locals_, rows, width, hidden, top):
        self.sizes = {"z": NZ, "x": groups // NZ, "y": locals_ // CORES, "c": CORES}
        self.groups, self.locals = groups, locals_
        self.devices = groups * locals_
        self.rows, self.width, self.hidden, self.top = rows, width, hidden, top
        self.cap = 2 * rows * top // self.devices
        self.widths = widths_of(width)
        self.chunks = len(self.widths)
        self.starts = [sum(self.widths[:c]) for c in range(self.chunks)]
        self.tokens = rows * self.devices
        self.half = self.tokens // CORES
        self.slots = self.devices // CORES * self.cap
        self.table = -(-3 * self.devices // 128) * 128
        self.peers = max(self.sizes.values()) - 1

    def order(self, chunk):
        return "zxyc" if chunk % 2 == 0 else "zyxc"

    def buffer_width(self, chunk):
        return self.widths[chunk] + (self.table if chunk < 2 else 0)

    def steps(self, chunk):
        out, step = [], 1
        for axis in self.order(chunk):
            out.append((axis, self.sizes[axis], step))
            step *= self.sizes[axis]
        return out


def bits(number):
    return number.bit_length() - 1


def kernel(plan, tok, ids, codes, wg, wu, wd, out, *scratch):
    p = plan
    nc = p.chunks
    rows = p.rows
    scratch = list(scratch)
    xbuf = [scratch.pop(0) for _ in range(nc)]
    rbuf = [[scratch.pop(0) for _ in range(4)] for _ in range(nc)]
    (gate_v, up_v, down_v, picked, gate_acc, up_acc, hid, scat, gath, slot_w, weighted,
     ag_send, ag_recv, rs_send, rs_recv, w_sem) = scratch

    g = lax.axis_index("group")
    l = lax.axis_index("local")
    me = g * p.locals + l
    nx = p.sizes["x"]
    at = {"z": g // nx, "x": g % nx, "y": l // CORES, "c": l % CORES}

    def peer(axis, k):
        spot = dict(at)
        spot[axis] = lax.rem(at[axis] + k, p.sizes[axis])
        return (spot["z"] * nx + spot["x"], spot["y"] * CORES + spot["c"]), spot[axis]

    loads = []
    for c in range(nc):
        span = pl.ds(p.starts[c], p.widths[c])
        pair = (
            pltpu.make_async_copy(wg.at[0, span, :], gate_v.at[span, :], w_sem.at[0, c]),
            pltpu.make_async_copy(wu.at[0, span, :], up_v.at[span, :], w_sem.at[1, c]),
        )
        for copy in pair:
            copy.start()
        loads.append(pair)
    down_load = pltpu.make_async_copy(wd.at[0], down_v, w_sem.at[2, 0])
    down_load.start()

    barrier = pltpu.get_barrier_semaphore()
    greeted = 0
    for axis in "zxyc":
        for k in range(1, p.sizes[axis]):
            pl.semaphore_signal(
                barrier, inc=1, device_id=peer(axis, k)[0], device_id_type=pl.DeviceIdType.MESH
            )
            greeted += 1

    lane = lax.broadcasted_iota(jnp.int32, (rows, p.table), 1)
    which = lane & (p.devices - 1)
    part = lane >> bits(p.devices)
    present = jnp.zeros((rows, p.table), F32)
    code = jnp.zeros((rows, p.table), jnp.int32)
    square = (rows, rows)
    diagonal = lax.broadcasted_iota(jnp.int32, square, 0) == lax.broadcasted_iota(
        jnp.int32, square, 1
    )

    def column(ref, k):
        spread = jnp.where(diagonal, ref[k : k + 1, :].astype(F32), 0.0)
        return jnp.sum(spread, axis=1, keepdims=True).astype(jnp.int32)

    for k in range(p.top):
        hit = column(ids, k) == which
        present = jnp.where(hit, 1.0, present)
        code = jnp.where(hit, column(codes, k), code)
    earlier = lax.broadcasted_iota(jnp.int32, (rows, rows), 0) > lax.broadcasted_iota(
        jnp.int32, (rows, rows), 1
    )
    before = jnp.dot(
        jnp.where(earlier, 1.0, 0.0).astype(BF), present.astype(BF), preferred_element_type=F32
    )
    live = jnp.logical_and(present > 0.5, before < p.cap - 0.5)
    rank = jnp.where(live, before, -1.0)
    high = jnp.where(live, (code >> 5).astype(F32), 0.0)
    low = jnp.where(live, (code & 31).astype(F32), 0.0)
    table = jnp.where(part == 0, rank, jnp.where(part == 1, high, low)).astype(BF)

    def base(c, j):
        total = 0
        for axis, size, step in p.steps(c)[j:]:
            total = total + at[axis] * step
        return total

    def span_of(start, count):
        return pl.ds(pl.multiple_of(start * rows, 16), count * rows)

    for c in range(nc):
        own = span_of(base(c, 0), 1)
        xbuf[c][own, : p.widths[c]] = tok[:, p.starts[c] : p.starts[c] + p.widths[c]]
        if c < 2:
            xbuf[c][own, p.widths[c] :] = table

    pl.semaphore_wait(barrier, greeted)

    def gather_copies(c, j):
        axis, size, step = p.steps(c)[j]
        span = span_of(base(c, j), step)
        copies = []
        for k in range(1, size):
            copies.append(
                pltpu.make_async_remote_copy(
                    src_ref=xbuf[c].at[span, :],
                    dst_ref=xbuf[c].at[span, :],
                    send_sem=ag_send.at[c, j, k - 1],
                    recv_sem=ag_recv.at[c, j, k - 1],
                    device_id=peer(axis, k)[0],
                    device_id_type=pl.DeviceIdType.MESH,
                )
            )
        return copies

    gathers = {}

    def gather_start(c, j):
        gathers[c, j] = gather_copies(c, j)
        for copy in gathers[c, j]:
            copy.start()

    def gather_wait(c, j):
        for copy in gathers[c, j]:
            copy.wait_recv()

    def one_hots(par):
        order = p.order(par)
        wide = p.widths[par]
        for core in range(CORES):
            tab = xbuf[par][core * p.half : (core + 1) * p.half, wide:].astype(F32)
            lanes = lax.broadcasted_iota(jnp.int32, (p.half, p.table), 1)
            rk = jnp.sum(jnp.where(lanes == me, tab, 0.0), axis=1, keepdims=True)
            row = lax.broadcasted_iota(jnp.int32, (p.half, p.slots), 0) >> bits(rows)
            spot = {}
            for axis in order[:3]:
                spot[axis] = row & (p.sizes[axis] - 1)
                row = row >> bits(p.sizes[axis])
            canon = (spot["y"] * p.sizes["x"] + spot["x"]) * p.sizes["z"] + spot["z"]
            slot = lax.broadcasted_iota(jnp.int32, (p.half, p.slots), 1)
            gap = (slot - canon * p.cap).astype(F32)
            hot = jnp.where(jnp.logical_and(gap == rk, rk > -0.5), 1.0, 0.0)
            scat[par, core * p.half : (core + 1) * p.half, :] = hot.astype(BF)
            turned = hot.T.astype(BF)
            gath[par, core] = turned
            if par == 0:
                tabs = jnp.dot(
                    turned,
                    xbuf[par][core * p.half : (core + 1) * p.half, wide:],
                    preferred_element_type=F32,
                )
                lanes = lax.broadcasted_iota(jnp.int32, (p.slots, p.table), 1)
                gate = jnp.where(lanes == p.devices + me, tabs * 32.0, 0.0)
                gate = gate + jnp.where(lanes == 2 * p.devices + me, tabs, 0.0)
                gate = jnp.sum(gate, axis=1, keepdims=True) * (1.0 / 1024.0)
                slot_w[core * p.slots : (core + 1) * p.slots, :] = jnp.broadcast_to(
                    gate, (p.slots, 128)
                )

    def into_hidden(c):
        par, wide = c % 2, p.widths[c]
        if c < 2:
            one_hots(par)
        for core in range(CORES):
            got = jnp.dot(
                gath[par, core],
                xbuf[c][core * p.half : (core + 1) * p.half, :wide],
                preferred_element_type=F32,
            )
            picked[core * p.slots : (core + 1) * p.slots, :wide] = got.astype(BF)
        for copy in loads[c]:
            copy.wait()
        depth = pl.ds(p.starts[c], wide)

        def tile(n, carry):
            cols = pl.ds(pl.multiple_of(n * 256, 256), 256)
            lhs = picked[:, :wide]
            a = jnp.dot(lhs, gate_v[depth, cols], preferred_element_type=F32)
            b = jnp.dot(lhs, up_v[depth, cols], preferred_element_type=F32)
            if c > 0:
                a = a + gate_acc[:, cols]
                b = b + up_acc[:, cols]
            if c == nc - 1:
                hid[:, cols] = (a / (1.0 + jnp.exp(-a)) * b).astype(BF)
            else:
                gate_acc[:, cols] = a
                up_acc[:, cols] = b
            return carry

        lax.fori_loop(0, p.hidden // 256, tile, 0)

    for c in range(nc):
        gather_start(c, 0)
    for t in range(nc + GATHER_LAG[3]):
        for j in (1, 2, 3):
            c = t - GATHER_LAG[j - 1]
            if 0 <= c < nc:
                gather_wait(c, j - 1)
                gather_start(c, j)
        c = t - GATHER_LAG[3]
        if 0 <= c < nc:
            gather_wait(c, 3)
            into_hidden(c)

    for c in range(nc):
        for j in range(4):
            for copy in gathers[c, j]:
                copy.wait_send()
    down_load.wait()

    sums = {}

    def sum_start(c, j):
        axis, size, step = p.steps(c)[j]
        outer = base(c, j + 1)
        copies = []
        for k in range(1, size):
            device, spot = peer(axis, k)
            copies.append(
                pltpu.make_async_remote_copy(
                    src_ref=xbuf[c].at[span_of(outer + spot * step, step), pl.ds(0, p.widths[c])],
                    dst_ref=rbuf[c][j].at[k - 1],
                    send_sem=rs_send.at[c, j, k - 1],
                    recv_sem=rs_recv.at[c, j, k - 1],
                    device_id=device,
                    device_id_type=pl.DeviceIdType.MESH,
                )
            )
        for copy in copies:
            copy.start()
        sums[c, j] = copies

    def sum_finish(c, j):
        axis, size, step = p.steps(c)[j]
        wide = p.widths[c]
        for copy in sums[c, j]:
            copy.wait_recv()
        start = base(c, j) * rows
        if j == 0:
            span = pl.ds(pl.multiple_of(start, 16), rows)
            total = xbuf[c][span, :wide].astype(F32)
            for k in range(size - 1):
                total = total + rbuf[c][j][k].astype(F32)
            out[:, p.starts[c] : p.starts[c] + wide] = total.astype(BF)
            return
        block = min(step * rows, 64)

        def add(i, carry):
            span = pl.ds(pl.multiple_of(start + i * block, 16), block)
            inner = pl.ds(pl.multiple_of(i * block, 16), block)
            if size == 2:
                xbuf[c][span, :wide] = xbuf[c][span, :wide] + rbuf[c][j][0, inner, :]
            else:
                total = xbuf[c][span, :wide].astype(F32)
                for k in range(size - 1):
                    total = total + rbuf[c][j][k, inner, :].astype(F32)
                xbuf[c][span, :wide] = total.astype(BF)
            return carry

        lax.fori_loop(0, step * rows // block, add, 0)

    def out_of_hidden(c):
        par, wide = c % 2, p.widths[c]

        def tile(n, carry):
            source = pl.ds(pl.multiple_of(p.starts[c] + n * 256, 256), 256)
            cols = pl.ds(pl.multiple_of(n * 256, 256), 256)
            made = jnp.dot(hid[...], down_v[:, source], preferred_element_type=F32)
            made = made * slot_w[:, :1]
            weighted[...] = made.astype(BF)
            for core in range(CORES):
                spread = jnp.dot(
                    scat[par, core * p.half : (core + 1) * p.half, :],
                    weighted[core * p.slots : (core + 1) * p.slots, :],
                    preferred_element_type=F32,
                )
                xbuf[c][core * p.half : (core + 1) * p.half, cols] = spread.astype(BF)
            return carry

        lax.fori_loop(0, wide // 256, tile, 0)

    for t in range(nc + SUM_LAG[3]):
        if t < nc:
            out_of_hidden(t)
            sum_start(t, 3)
        for lag, j in zip(SUM_LAG, (3, 2, 1, 0)):
            c = t - lag
            if 0 <= c < nc:
                sum_finish(c, j)
                if j > 0:
                    sum_start(c, j - 1)
    for c in range(nc):
        for j in range(4):
            for copy in sums[c, j]:
                copy.wait_send()


def local(tokens, expert_ids, gate_codes, w_gate, w_up, w_down):
    rows, width = tokens.shape
    hidden = w_gate.shape[2]
    p = Plan(
        lax.axis_size("group"), lax.axis_size("local"), rows, width, hidden, expert_ids.shape[1]
    )
    nc = p.chunks
    wide = max(p.widths)
    shapes = [pltpu.VMEM((p.tokens, p.buffer_width(c)), BF) for c in range(nc)]
    for c in range(nc):
        for axis, size, step in p.steps(c):
            shapes.append(pltpu.VMEM((size - 1, step * rows, p.widths[c]), BF))
    slots = CORES * p.slots
    sems = pltpu.SemaphoreType.DMA((nc, 4, p.peers))
    shapes += [
        pltpu.VMEM((width, hidden), BF),
        pltpu.VMEM((width, hidden), BF),
        pltpu.VMEM((hidden, width), BF),
        pltpu.VMEM((slots, wide), BF),
        pltpu.VMEM((slots, hidden), F32),
        pltpu.VMEM((slots, hidden), F32),
        pltpu.VMEM((slots, hidden), BF),
        pltpu.VMEM((2, p.tokens, p.slots), BF),
        pltpu.VMEM((2, CORES, p.slots, p.half), BF),
        pltpu.VMEM((slots, 128), F32),
        pltpu.VMEM((slots, 256), BF),
        sems, sems, sems, sems,
        pltpu.SemaphoreType.DMA((3, nc)),
    ]
    vmem = pl.BlockSpec(memory_space=pltpu.VMEM)
    hbm = pl.BlockSpec(memory_space=pl.ANY)
    return pl.pallas_call(
        functools.partial(kernel, p),
        out_shape=jax.ShapeDtypeStruct((rows, width), BF),
        in_specs=[vmem, vmem, vmem, hbm, hbm, hbm],
        out_specs=vmem,
        scratch_shapes=shapes,
        compiler_params=pltpu.CompilerParams(
            collective_id=0, has_side_effects=True, vmem_limit_bytes=62 * 1024 * 1024
        ),
        cost_estimate=pl.CostEstimate(
            flops=6 * slots * width * hidden, bytes_accessed=6 * width * hidden, transcendentals=0
        ),
    )(tokens, expert_ids.T, gate_codes.T, w_gate, w_up, w_down)


def solution(mesh):
    placed = (
        P(("group", "local"), None),
        P(("group", "local"), None),
        P(("group", "local"), None),
        P(("group", "local"), None, None),
        P(("group", "local"), None, None),
        P(("group", "local"), None, None),
    )
    return jax.shard_map(
        local, mesh=mesh, in_specs=placed, out_specs=P(("group", "local"), None), check_vma=False
    )
```

```python
import functools

import jax
import jax.numpy as jnp
from jax import lax
from jax.experimental import pallas as pl
from jax.experimental.pallas import tpu as pltpu
from jax.sharding import PartitionSpec as P

BF = jnp.bfloat16
F32 = jnp.float32
NZ = 4
CORES = 2
GATHER_LAG = (0, 2, 4, 5)
SUM_LAG = (2, 4, 6, 8)


def widths_of(width):
    first = 256
    return [first] * 2 + [(width - 2 * first) // 4] * 4


class Plan:
    def __init__(self, groups, locals_, rows, width, hidden, top):
        self.sizes = {"z": NZ, "x": groups // NZ, "y": locals_ // CORES, "c": CORES}
        self.groups, self.locals = groups, locals_
        self.devices = groups * locals_
        self.rows, self.width, self.hidden, self.top = rows, width, hidden, top
        self.cap = 2 * rows * top // self.devices
        self.widths = widths_of(width)
        self.chunks = len(self.widths)
        self.starts = [sum(self.widths[:c]) for c in range(self.chunks)]
        self.tokens = rows * self.devices
        self.half = self.tokens // CORES
        self.slots = self.devices // CORES * self.cap
        self.table = -(-3 * self.devices // 128) * 128
        self.peers = max(self.sizes.values()) - 1

    def order(self, chunk):
        return "zxyc" if chunk % 2 == 0 else "zyxc"

    def buffer_width(self, chunk):
        return self.widths[chunk] + (self.table if chunk < 2 else 0)

    def steps(self, chunk):
        out, step = [], 1
        for axis in self.order(chunk):
            out.append((axis, self.sizes[axis], step))
            step *= self.sizes[axis]
        return out


def bits(number):
    return number.bit_length() - 1


def kernel(plan, tok, ids, codes, wg, wu, wd, out, *scratch):
    p = plan
    nc = p.chunks
    rows = p.rows
    scratch = list(scratch)
    xbuf = [scratch.pop(0) for _ in range(nc)]
    rbuf = [[scratch.pop(0) for _ in range(4)] for _ in range(nc)]
    (gate_v, up_v, down_v, picked, gate_acc, up_acc, hid, scat, gath, slot_w, weighted,
     ag_send, ag_recv, rs_send, rs_recv, w_sem) = scratch

    g = lax.axis_index("group")
    l = lax.axis_index("local")
    me = g * p.locals + l
    nx = p.sizes["x"]
    at = {"z": g // nx, "x": g % nx, "y": l // CORES, "c": l % CORES}

    def peer(axis, k):
        spot = dict(at)
        spot[axis] = lax.rem(at[axis] + k, p.sizes[axis])
        return (spot["z"] * nx + spot["x"], spot["y"] * CORES + spot["c"]), spot[axis]

    loads = []
    for c in range(nc):
        span = pl.ds(p.starts[c], p.widths[c])
        pair = (
            pltpu.make_async_copy(wg.at[0, span, :], gate_v.at[span, :], w_sem.at[0, c]),
            pltpu.make_async_copy(wu.at[0, span, :], up_v.at[span, :], w_sem.at[1, c]),
        )
        for copy in pair:
            copy.start()
        loads.append(pair)
    down_load = pltpu.make_async_copy(wd.at[0], down_v, w_sem.at[2, 0])
    down_load.start()

    barrier = pltpu.get_barrier_semaphore()
    greeted = 0
    for axis in "zxyc":
        for k in range(1, p.sizes[axis]):
            pl.semaphore_signal(
                barrier, inc=1, device_id=peer(axis, k)[0], device_id_type=pl.DeviceIdType.MESH
            )
            greeted += 1

    lane = lax.broadcasted_iota(jnp.int32, (rows, p.table), 1)
    which = lane & (p.devices - 1)
    part = lane >> bits(p.devices)
    present = jnp.zeros((rows, p.table), F32)
    code = jnp.zeros((rows, p.table), jnp.int32)
    square = (rows, rows)
    diagonal = lax.broadcasted_iota(jnp.int32, square, 0) == lax.broadcasted_iota(
        jnp.int32, square, 1
    )

    def column(ref, k):
        spread = jnp.where(diagonal, ref[k : k + 1, :].astype(F32), 0.0)
        return jnp.sum(spread, axis=1, keepdims=True).astype(jnp.int32)

    for k in range(p.top):
        hit = column(ids, k) == which
        present = jnp.where(hit, 1.0, present)
        code = jnp.where(hit, column(codes, k), code)
    earlier = lax.broadcasted_iota(jnp.int32, (rows, rows), 0) > lax.broadcasted_iota(
        jnp.int32, (rows, rows), 1
    )
    before = jnp.dot(
        jnp.where(earlier, 1.0, 0.0).astype(BF), present.astype(BF), preferred_element_type=F32
    )
    live = jnp.logical_and(present > 0.5, before < p.cap - 0.5)
    rank = jnp.where(live, before, -1.0)
    high = jnp.where(live, (code >> 5).astype(F32), 0.0)
    low = jnp.where(live, (code & 31).astype(F32), 0.0)
    table = jnp.where(part == 0, rank, jnp.where(part == 1, high, low)).astype(BF)

    def base(c, j):
        total = 0
        for axis, size, step in p.steps(c)[j:]:
            total = total + at[axis] * step
        return total

    def span_of(start, count):
        return pl.ds(pl.multiple_of(start * rows, 16), count * rows)

    for c in range(nc):
        own = span_of(base(c, 0), 1)
        xbuf[c][own, : p.widths[c]] = tok[:, p.starts[c] : p.starts[c] + p.widths[c]]
        if c < 2:
            xbuf[c][own, p.widths[c] :] = table

    pl.semaphore_wait(barrier, greeted)

    def gather_copies(c, j):
        axis, size, step = p.steps(c)[j]
        span = span_of(base(c, j), step)
        copies = []
        for k in range(1, size):
            copies.append(
                pltpu.make_async_remote_copy(
                    src_ref=xbuf[c].at[span, :],
                    dst_ref=xbuf[c].at[span, :],
                    send_sem=ag_send.at[c, j, k - 1],
                    recv_sem=ag_recv.at[c, j, k - 1],
                    device_id=peer(axis, k)[0],
                    device_id_type=pl.DeviceIdType.MESH,
                )
            )
        return copies

    gathers = {}

    def gather_start(c, j):
        gathers[c, j] = gather_copies(c, j)
        for copy in gathers[c, j]:
            copy.start()

    def gather_wait(c, j):
        for copy in gathers[c, j]:
            copy.wait_recv()

    def one_hots(par):
        order = p.order(par)
        wide = p.widths[par]
        for core in range(CORES):
            tab = xbuf[par][core * p.half : (core + 1) * p.half, wide:].astype(F32)
            lanes = lax.broadcasted_iota(jnp.int32, (p.half, p.table), 1)
            rk = jnp.sum(jnp.where(lanes == me, tab, 0.0), axis=1, keepdims=True)
            row = lax.broadcasted_iota(jnp.int32, (p.half, p.slots), 0) >> bits(rows)
            spot = {}
            for axis in order[:3]:
                spot[axis] = row & (p.sizes[axis] - 1)
                row = row >> bits(p.sizes[axis])
            canon = (spot["y"] * p.sizes["x"] + spot["x"]) * p.sizes["z"] + spot["z"]
            slot = lax.broadcasted_iota(jnp.int32, (p.half, p.slots), 1)
            gap = (slot - canon * p.cap).astype(F32)
            hot = jnp.where(jnp.logical_and(gap == rk, rk > -0.5), 1.0, 0.0)
            scat[par, core * p.half : (core + 1) * p.half, :] = hot.astype(BF)
            turned = hot.T.astype(BF)
            gath[par, core] = turned
            if par == 0:
                tabs = jnp.dot(
                    turned,
                    xbuf[par][core * p.half : (core + 1) * p.half, wide:],
                    preferred_element_type=F32,
                )
                lanes = lax.broadcasted_iota(jnp.int32, (p.slots, p.table), 1)
                gate = jnp.where(lanes == p.devices + me, tabs * 32.0, 0.0)
                gate = gate + jnp.where(lanes == 2 * p.devices + me, tabs, 0.0)
                gate = jnp.sum(gate, axis=1, keepdims=True) * (1.0 / 1024.0)
                slot_w[core * p.slots : (core + 1) * p.slots, :] = jnp.broadcast_to(
                    gate, (p.slots, 128)
                )

    def into_hidden(c):
        par, wide = c % 2, p.widths[c]
        if c < 2:
            one_hots(par)
        for core in range(CORES):
            got = jnp.dot(
                gath[par, core],
                xbuf[c][core * p.half : (core + 1) * p.half, :wide],
                preferred_element_type=F32,
            )
            picked[core * p.slots : (core + 1) * p.slots, :wide] = got.astype(BF)
        for copy in loads[c]:
            copy.wait()
        depth = pl.ds(p.starts[c], wide)

        def tile(n, carry):
            cols = pl.ds(pl.multiple_of(n * 256, 256), 256)
            lhs = picked[:, :wide]
            a = jnp.dot(lhs, gate_v[depth, cols], preferred_element_type=F32)
            b = jnp.dot(lhs, up_v[depth, cols], preferred_element_type=F32)
            if c > 0:
                a = a + gate_acc[:, cols]
                b = b + up_acc[:, cols]
            if c == nc - 1:
                hid[:, cols] = (a / (1.0 + jnp.exp(-a)) * b).astype(BF)
            else:
                gate_acc[:, cols] = a
                up_acc[:, cols] = b
            return carry

        lax.fori_loop(0, p.hidden // 256, tile, 0)

    for c in range(nc):
        gather_start(c, 0)
    for t in range(nc + GATHER_LAG[3]):
        for j in (1, 2, 3):
            c = t - GATHER_LAG[j - 1]
            if 0 <= c < nc:
                gather_wait(c, j - 1)
                gather_start(c, j)
        c = t - GATHER_LAG[3]
        if 0 <= c < nc:
            gather_wait(c, 3)
            into_hidden(c)

    for c in range(nc):
        for j in range(4):
            for copy in gathers[c, j]:
                copy.wait_send()
    down_load.wait()

    sums = {}

    def sum_start(c, j):
        axis, size, step = p.steps(c)[j]
        outer = base(c, j + 1)
        copies = []
        for k in range(1, size):
            device, spot = peer(axis, k)
            copies.append(
                pltpu.make_async_remote_copy(
                    src_ref=xbuf[c].at[span_of(outer + spot * step, step), pl.ds(0, p.widths[c])],
                    dst_ref=rbuf[c][j].at[k - 1],
                    send_sem=rs_send.at[c, j, k - 1],
                    recv_sem=rs_recv.at[c, j, k - 1],
                    device_id=device,
                    device_id_type=pl.DeviceIdType.MESH,
                )
            )
        for copy in copies:
            copy.start()
        sums[c, j] = copies

    def sum_finish(c, j):
        axis, size, step = p.steps(c)[j]
        wide = p.widths[c]
        for copy in sums[c, j]:
            copy.wait_recv()
        start = base(c, j) * rows
        if j == 0:
            span = pl.ds(pl.multiple_of(start, 16), rows)
            total = xbuf[c][span, :wide].astype(F32)
            for k in range(size - 1):
                total = total + rbuf[c][j][k].astype(F32)
            out[:, p.starts[c] : p.starts[c] + wide] = total.astype(BF)
            return
        block = min(step * rows, 64)

        def add(i, carry):
            span = pl.ds(pl.multiple_of(start + i * block, 16), block)
            inner = pl.ds(pl.multiple_of(i * block, 16), block)
            if size == 2:
                xbuf[c][span, :wide] = xbuf[c][span, :wide] + rbuf[c][j][0, inner, :]
            else:
                total = xbuf[c][span, :wide].astype(F32)
                for k in range(size - 1):
                    total = total + rbuf[c][j][k, inner, :].astype(F32)
                xbuf[c][span, :wide] = total.astype(BF)
            return carry

        lax.fori_loop(0, step * rows // block, add, 0)

    def out_of_hidden(c):
        par, wide = c % 2, p.widths[c]

        def tile(n, carry):
            source = pl.ds(pl.multiple_of(p.starts[c] + n * 256, 256), 256)
            cols = pl.ds(pl.multiple_of(n * 256, 256), 256)
            made = jnp.dot(hid[...], down_v[:, source], preferred_element_type=F32)
            made = made * slot_w[:, :1]
            weighted[...] = made.astype(BF)
            for core in range(CORES):
                spread = jnp.dot(
                    scat[par, core * p.half : (core + 1) * p.half, :],
                    weighted[core * p.slots : (core + 1) * p.slots, :],
                    preferred_element_type=F32,
                )
                xbuf[c][core * p.half : (core + 1) * p.half, cols] = spread.astype(BF)
            return carry

        lax.fori_loop(0, wide // 256, tile, 0)

    for t in range(nc + SUM_LAG[3]):
        if t < nc:
            out_of_hidden(t)
            sum_start(t, 3)
        for lag, j in zip(SUM_LAG, (3, 2, 1, 0)):
            c = t - lag
            if 0 <= c < nc:
                sum_finish(c, j)
                if j > 0:
                    sum_start(c, j - 1)
    for c in range(nc):
        for j in range(4):
            for copy in sums[c, j]:
                copy.wait_send()


def local(tokens, expert_ids, gate_codes, w_gate, w_up, w_down):
    rows, width = tokens.shape
    hidden = w_gate.shape[2]
    p = Plan(
        lax.axis_size("group"), lax.axis_size("local"), rows, width, hidden, expert_ids.shape[1]
    )
    nc = p.chunks
    wide = max(p.widths)
    shapes = [pltpu.VMEM((p.tokens, p.buffer_width(c)), BF) for c in range(nc)]
    for c in range(nc):
        for axis, size, step in p.steps(c):
            shapes.append(pltpu.VMEM((size - 1, step * rows, p.widths[c]), BF))
    slots = CORES * p.slots
    sems = pltpu.SemaphoreType.DMA((nc, 4, p.peers))
    shapes += [
        pltpu.VMEM((width, hidden), BF),
        pltpu.VMEM((width, hidden), BF),
        pltpu.VMEM((hidden, width), BF),
        pltpu.VMEM((slots, wide), BF),
        pltpu.VMEM((slots, hidden), F32),
        pltpu.VMEM((slots, hidden), F32),
        pltpu.VMEM((slots, hidden), BF),
        pltpu.VMEM((2, p.tokens, p.slots), BF),
        pltpu.VMEM((2, CORES, p.slots, p.half), BF),
        pltpu.VMEM((slots, 128), F32),
        pltpu.VMEM((slots, 256), BF),
        sems, sems, sems, sems,
        pltpu.SemaphoreType.DMA((3, nc)),
    ]
    vmem = pl.BlockSpec(memory_space=pltpu.VMEM)
    hbm = pl.BlockSpec(memory_space=pl.ANY)
    return pl.pallas_call(
        functools.partial(kernel, p),
        out_shape=jax.ShapeDtypeStruct((rows, width), BF),
        in_specs=[vmem, vmem, vmem, hbm, hbm, hbm],
        out_specs=vmem,
        scratch_shapes=shapes,
        compiler_params=pltpu.CompilerParams(
            collective_id=0, has_side_effects=True, vmem_limit_bytes=62 * 1024 * 1024
        ),
        cost_estimate=pl.CostEstimate(
            flops=6 * slots * width * hidden, bytes_accessed=6 * width * hidden, transcendentals=0
        ),
    )(tokens, expert_ids.T, gate_codes.T, w_gate, w_up, w_down)


def solution(mesh):
    placed = (
        P(("group", "local"), None),
        P(("group", "local"), None),
        P(("group", "local"), None),
        P(("group", "local"), None, None),
        P(("group", "local"), None, None),
        P(("group", "local"), None, None),
    )
    return jax.shard_map(
        local, mesh=mesh, in_specs=placed, out_specs=P(("group", "local"), None), check_vma=False
    )
```
